32 devices in a mesh: groups: 2 (over y), section: 2 (over core), expert: 8 (over z, x).
Axes of the slice: x: 2, y: 2, z: 4, core: 2. Of those that a mesh axis runs over, the one named last changes fastest.
Arguments:
- hidden_in: bfloat16 [2, 32, 3584], P(None, ('groups', 'expert')), parts along dimension 1, may hold values from -6 to 6
- norm_gain: float32 [2, 3584], P('section'), may hold values from 0.1 to 1.9
- gate_weight: bfloat16 [2, 3584, 1024], P('section', None, 'expert'), may hold values from -0.09375 to 0.09375
- up_weight: bfloat16 [2, 3584, 1024], P('section', None, 'expert'), may hold values from -0.09375 to 0.09375
- down_weight: bfloat16 [2, 1024, 3584], P('section', 'expert'), may hold values from -0.5 to 0.5
- routes: int32 [2, 2, 32, 4], P('section', None, ('groups', 'expert')), parts along dimension 2, may hold values from 0 to 7, all different within a row; in each aligned block of 2 rows (0 to 1, 2 to 3, ..., all dimensions but the last counted through in order) at most 2 rows name the same one
- route_weights: float32 [2, 2, 32, 4], P('section', None, ('groups', 'expert')), parts along dimension 2, may hold values from 0.2 to 1
- queries: bfloat16 [2, 2, 32, 64, 576], P('section', None, ('groups', 'expert')), parts along dimension 2, may hold values from -18 to 18
- latent_cache: bfloat16 [2, 2, 32, 64, 576], P('section', None, ('groups', 'expert')), parts along dimension 2, may hold values from -4.5 to 4.5
- lengths: int32 [2, 32], P(None, ('groups', 'expert')), parts along dimension 1, may hold values from 16 to 64, as said below
Outputs:
- layer_out: bfloat16 [2, 2, 32, 3584], P('section', None, ('groups', 'expert')), parts along dimension 2
- attention_out: bfloat16 [2, 2, 32, 64, 512], P('section', None, ('groups', 'expert')), parts along dimension 2
The draws below stay inside these ranges and needn't reach their ends.
There are 2 independent parts, one for each index of `groups`. The reference program is written for one: setup_inputs(seed, part) draws one part's arguments, and reference() takes and returns one part's arrays. A program takes and returns all parts, laid end to end along the dimension named above; an argument that names none is the same for every part. Nothing has to cross between parts.
Inputs may be any that keep to these rules, and one draw needn't show every extreme that they name: `routes`: each row names 4 different experts; in every aligned block of 2 rows of one layer and micro-batch no expert is named by more than 2 rows, and in some blocks some expert is named by exactly 2. `lengths`: in every block of 2 rows the first row has length 64.
All inputs are finite; a program needn't handle non-finite values.
Results may differ from the reference program's by a relative error of at most 0.007.
Values may be sent and summed in bfloat16 or wider, within the bound.
A program may use at most 64 MiB of HBM per device.

```python
import math
import jax
import jax.numpy as jnp
import numpy as np
from jax import lax

D = 3584
F_DEV = 128
EXPERTS = 8
TOPK = 4
HEADS = 64
LAT = 512
ROPE = 64
CTX = 64
R = 2
MICRO = 2
CAP = 2
FF = 128
ROWS = 16
N_SECTION = 2
N_EXPERT = 8


def cache_values(key):
    base = jnp.clip(jax.random.normal(key, (N_SECTION, MICRO, ROWS, CTX, LAT + ROPE), jnp.float32), -3.5, 3.5)
    second = base[:, :, :, 1, :]
    return base.at[:, :, :, 1, :].set(second)


def draw_latent_cache(key, part):
    return cache_values(key).astype(jnp.bfloat16)


def draw_queries(key, part):
    key = jax.random.fold_in(key, 5)
    first_key = jax.random.fold_in(key, 0)
    shape = (N_SECTION, MICRO, ROWS, HEADS, LAT + ROPE)
    values = jnp.clip(jax.random.normal(first_key, shape, jnp.float32), -4.0, 4.0)
    return values.astype(jnp.bfloat16)


def draw_lengths(key, part):
    key = jax.random.fold_in(key, 7)
    values = jax.random.randint(key, (MICRO, ROWS), CTX // 4, CTX + 1, jnp.int32)
    leading = (jnp.arange(ROWS) % R == 0)[None, :]
    return jnp.where(leading, CTX, values).astype(jnp.int32)


def block_levels(key, extent, cuts, low, top_value):
    def one(position, shards_of):
        steps = jax.random.uniform(jax.random.fold_in(jax.random.fold_in(key, 6), position), (shards_of,), jnp.float32, low / len(cuts), top_value / len(cuts))
        return jnp.repeat(jnp.exp(steps), extent[position] // shards_of).reshape((-1,) + (1,) * (len(extent) - position - 1))

    gain = one(*cuts[0])
    for cut in cuts[1:]:
        gain = gain * one(*cut)
    return gain


def routed_block(rng, own, number, rows, number_of, top, most, lean):
    order = jax.random.permutation(rng, number_of)
    heavy_load, ordinary = portions_of(number_of, rows * top, most, lean, True), portions_of(number_of, rows * top, most, lean, False)
    places = jnp.arange(number_of)

    def named(sizes, rotation):
        used = int((sizes > 0).sum())
        fixed = max(1, used // 4)
        moved = fixed + (places - fixed + rotation * (used - fixed)) % max(1, number_of - fixed)
        return jnp.zeros((number_of,), jnp.int32).at[order[jnp.where(places < fixed, places, moved)]].set(jnp.asarray(sizes, jnp.int32))

    sizes = jnp.where(number % 4 == 0, named(heavy_load, number // 4), named(ordinary, number - number // 4 - 1))
    mixed = jax.random.permutation(jax.random.fold_in(own, 3), number_of)
    giver, sink = mixed[0:number_of // 2 * 2:2], mixed[1:number_of // 2 * 2:2]
    room = jnp.minimum(sizes[giver] - 1, most - sizes[sink]) // 2
    room = jnp.where((giver == order[0]) | (sink == order[0]) | (sizes[sink] == 0), 0, jnp.maximum(room, 0))
    moved = jax.random.randint(jax.random.fold_in(own, 4), (number_of // 2,), 0, 1 << 20) % (room + 1)
    sizes = sizes.at[giver].add(-moved).at[sink].add(moved)
    members = jnp.searchsorted(jnp.cumsum(sizes), jnp.arange(rows * top), side="right").astype(jnp.int32)
    listing = members.reshape(top, rows).T
    listing = listing[jax.random.permutation(jax.random.fold_in(own, 1), rows)]
    rotation = jax.random.randint(jax.random.fold_in(own, 2), (rows, 1), 0, top)
    return jnp.take_along_axis(listing, (jnp.arange(top)[None, :] + rotation) % top, axis=1)


def portions_of(count, total, limit, slope, full):
    portions = [(1 << 20) // math.isqrt(standing ** slope) + 1 for standing in range(1, count + 1)]
    largest = limit if full else min(limit, max(-(-total // count), total * portions[0] // sum(portions)))
    least = 1 if total - largest >= count - 1 else 0
    given, rest = [largest] + [least] * (count - 1), total - largest - least * (count - 1)
    while rest > 0:
        movable = [i for i in range(1, count) if given[i] < largest] or [i for i in range(1, count) if given[i] < limit]
        whole, budget = sum([portions[i] for i in movable]), rest
        for i in movable:
            more = min(limit - given[i], max(1, budget * portions[i] // whole), rest)
            given[i] = given[i] + more
            rest = rest - more
    return np.array(given)


def noise(stream_key, extent, spread, most, cuts=(), kind=jnp.bfloat16):
    factor_of = block_levels(stream_key, extent, cuts, -0.22, 0.18) if cuts else 1.0
    drawn = jax.random.normal(stream_key, extent, jnp.float32) * spread * factor_of
    return jnp.minimum(jnp.maximum(drawn, -most), most).astype(kind)


def setup_inputs(seed: int = 0, part: int = 0) -> dict:
    arg_keys = jax.random.split(jax.random.key(seed), 11)
    part_splits = jax.random.split(jax.random.fold_in(arg_keys[10], part), 11)
    hidden_in = noise(part_splits[0], (MICRO, ROWS, D), 1.0, 6.0, ((1, 8),))
    norm_gain = jnp.clip(1.0 + 0.18 * jax.random.normal(arg_keys[1], (N_SECTION, D), jnp.float32), 0.1, 1.9)
    gate_weight = noise(arg_keys[2], (N_SECTION, D, EXPERTS * FF), D ** -0.5, 0.09375, ((0, 2), (2, 8)))
    up_weight = noise(arg_keys[3], (N_SECTION, D, EXPERTS * FF), D ** -0.5, 0.09375, ((0, 2), (2, 8)))
    down_weight = noise(arg_keys[4], (N_SECTION, EXPERTS * FF, D), FF ** -0.5, 0.5, ((0, 2), (1, 8)))
    routes_keys = jax.random.split(jax.random.fold_in(part_splits[5], 1), N_SECTION * MICRO * ROWS // R)
    routes_turns = jax.random.permutation(jax.random.fold_in(part_splits[5], 3), N_SECTION * MICRO * ROWS // R)
    routes = jax.vmap(lambda own, number: routed_block(jax.random.fold_in(part_splits[5], 2), own, number, R, EXPERTS, TOPK, CAP, 2))(routes_keys, routes_turns).reshape((N_SECTION, MICRO, ROWS, TOPK))
    route_weights = jnp.clip(0.2 + 0.8 * jax.random.uniform(part_splits[6], (N_SECTION, MICRO, ROWS, TOPK), jnp.float32) ** block_levels(part_splits[6], (N_SECTION, MICRO, ROWS, TOPK), ((0, 2), (2, 8)), -0.2, 0.2), 0.2, 1.0)
    queries = draw_queries(jax.random.fold_in(jax.random.fold_in(arg_keys[10], part), 71), part)
    latent_cache = draw_latent_cache(jax.random.fold_in(jax.random.fold_in(arg_keys[10], part), 71), part)
    lengths = draw_lengths(jax.random.fold_in(jax.random.fold_in(arg_keys[10], part), 71), part)
    return {"hidden_in": hidden_in, "norm_gain": norm_gain, "gate_weight": gate_weight, "up_weight": up_weight, "down_weight": down_weight, "routes": routes, "route_weights": route_weights, "queries": queries, "latent_cache": latent_cache, "lengths": lengths}


att_scale = 0.07216878364870322

def rms_normed(wide_input, norm_scale):
    mean_square = lax.optimization_barrier(jnp.mean(wide_input * wide_input, axis=-1, keepdims=True))
    return (wide_input * lax.rsqrt(mean_square + 1e-06) * norm_scale).astype(jnp.bfloat16)

def pair_slots(route_blocks):
    onehot = (route_blocks[..., None] == jnp.arange(EXPERTS, dtype=jnp.int32)).astype(jnp.int32)
    earlier = jnp.cumsum(onehot, axis=1) - onehot
    return lax.optimization_barrier(jnp.sum(earlier * onehot, axis=-1)).astype(jnp.int32)

def moe_layer(hidden, norm_scale, w_gate, w_up, w_down, route_now, weight_now):
    wide_input = hidden.astype(jnp.float32)
    normed = rms_normed(wide_input, norm_scale)
    route_blocks = route_now.reshape(N_EXPERT, R * TOPK)
    slot_index = pair_slots(route_blocks)
    block_rows = normed.reshape(N_EXPERT, R, D).astype(jnp.float32)
    group_size = N_EXPERT // EXPERTS

    def one_expert(expert_id):
        selected = (route_blocks == expert_id)[..., None] & (slot_index[..., None] == jnp.arange(CAP, dtype=jnp.int32))
        selected = lax.optimization_barrier(jnp.sum(selected.reshape(N_EXPERT, R, TOPK, CAP).astype(jnp.float32), axis=2))
        buffer_rows = jnp.einsum('nrc,nrd->ncd', selected, block_rows).astype(jnp.bfloat16).reshape(N_EXPERT * CAP, D)
        gate_cols = lax.dynamic_slice_in_dim(w_gate, expert_id * FF, FF, 1)
        up_cols = lax.dynamic_slice_in_dim(w_up, expert_id * FF, FF, 1)
        gate_proj = jnp.dot(buffer_rows, gate_cols, preferred_element_type=jnp.float32)
        up_proj = jnp.dot(buffer_rows, up_cols, preferred_element_type=jnp.float32)
        activation = (jax.nn.silu(gate_proj) * up_proj).astype(jnp.bfloat16)
        down_rows = lax.dynamic_slice_in_dim(w_down, expert_id * FF, FF, 0).reshape(group_size, F_DEV, D)
        partial_terms = jnp.einsum('sgf,gfd->sgd', activation.reshape(-1, group_size, F_DEV).astype(jnp.float32), down_rows.astype(jnp.float32)).astype(jnp.bfloat16)
        return lax.optimization_barrier(jnp.sum(partial_terms.astype(jnp.float32), axis=1)).reshape(N_EXPERT, CAP, D)
    expert_out = lax.map(one_expert, jnp.arange(EXPERTS, dtype=jnp.int32))
    block_ids = jnp.arange(N_EXPERT, dtype=jnp.int32)[:, None]
    picked = expert_out[route_blocks, block_ids, slot_index].reshape(ROWS, TOPK, D)
    combined = lax.optimization_barrier(jnp.sum(weight_now[..., None] * picked, axis=1))
    return (wide_input + combined).astype(jnp.bfloat16)

def attend(query_rows, cache_rows, length_rows):
    query_wide = query_rows.astype(jnp.float32)
    cache_wide = cache_rows.astype(jnp.float32)
    scores = jnp.einsum('rhc,rlc->rhl', query_wide, cache_wide) * att_scale
    visible = jnp.arange(CTX, dtype=jnp.int32)[None, None, :] < length_rows[:, None, None]
    scores = jnp.where(visible, scores, -jnp.inf)
    row_maximum = lax.optimization_barrier(jnp.max(scores, axis=-1, keepdims=True))
    expanded = jnp.exp(scores - row_maximum)
    probabilities = (expanded / lax.optimization_barrier(jnp.sum(expanded, axis=-1, keepdims=True))).astype(jnp.bfloat16)
    return jnp.einsum('rhl,rlc->rhc', probabilities.astype(jnp.float32), cache_wide[..., :LAT]).astype(jnp.bfloat16)

def reference(hidden_in, norm_gain, gate_weight, up_weight, down_weight, routes, route_weights, queries, latent_cache, lengths):
    first_layer = []
    second_layer = []
    for batch in range(MICRO):
        first_out = moe_layer(hidden_in[batch], norm_gain[0], gate_weight[0], up_weight[0], down_weight[0], routes[0, batch], route_weights[0, batch])
        first_layer.append(first_out)
        second_layer.append(moe_layer(first_out, norm_gain[1], gate_weight[1], up_weight[1], down_weight[1], routes[1, batch], route_weights[1, batch]))
    layer_out = jnp.stack([jnp.stack(first_layer), jnp.stack(second_layer)])
    attention_out = jnp.stack([jnp.stack([attend(queries[layer, batch], latent_cache[layer, batch], lengths[batch]) for batch in range(MICRO)]) for layer in range(N_SECTION)])
    return (layer_out, attention_out)
```

```python
import functools

import jax
import jax.numpy as jnp
from jax import lax
from jax.experimental import pallas as pl
from jax.experimental.pallas import tpu as pltpu
from jax.sharding import PartitionSpec as P

EXPERTS = 8
LAT = 512
FOLD = 4

att_scale = 0.07216878364870322


def loop(count, body):
    if count <= 8:
        for step in range(count):
            body(step)
    else:

        @pl.loop(0, count)
        def _(step):
            body(step)


def kernel(
    n,
    hid,
    gain,
    wg,
    wu,
    wd,
    routes,
    rweights,
    queries,
    cache,
    lens,
    lo,
    ao,
    xs,
    g16,
    rt16,
    rw16,
    tab,
    tab_in,
    sbuf,
    disp,
    pout,
    ret,
    xb,
    xb_in,
    wgu_v,
    wd_v,
    q_v,
    c_v,
    ao_v,
    load_sem,
    out_sem,
    d_send,
    d_recv,
    r_send,
    r_recv,
    t_send,
    t_recv,
    x_send,
    x_recv,
):
    sec = lax.axis_index("section")
    me = lax.axis_index("expert")
    micro, rows, width = hid.shape
    fold = width // FOLD
    per = micro * rows
    tall = FOLD * per
    hidden_units = wg.shape[2]
    group = n // EXPERTS

    loads = [
        pltpu.make_async_copy(wg.at[0], wgu_v.at[:, pl.ds(0, hidden_units)], load_sem.at[0]),
        pltpu.make_async_copy(
            wu.at[0], wgu_v.at[:, pl.ds(hidden_units, hidden_units)], load_sem.at[1]
        ),
        pltpu.make_async_copy(wd.at[0], wd_v, load_sem.at[2]),
        pltpu.make_async_copy(queries.at[0], q_v, load_sem.at[3]),
        pltpu.make_async_copy(cache.at[0], c_v, load_sem.at[4]),
    ]
    for copy in loads:
        copy.start()

    barrier = pltpu.get_barrier_semaphore()

    def greet(step):
        other = lax.rem(me + step + 1, n)
        pl.semaphore_signal(
            barrier, inc=1, device_id={"expert": other}, device_id_type=pl.DeviceIdType.MESH
        )

    def greet_across(step):
        other = lax.rem(me + step, n)
        pl.semaphore_signal(
            barrier,
            inc=1,
            device_id={"section": 1 - sec, "expert": other},
            device_id_type=pl.DeviceIdType.MESH,
        )

    loop(n - 1, greet)
    loop(n, greet_across)

    for q in range(FOLD):
        columns = pl.ds(q * fold, fold)
        g16[pl.ds(q * per, per), :] = jnp.broadcast_to(gain[:, columns], (per, fold))
        for m in range(micro):
            at = pl.ds(q * per + m * rows, rows)
            xs[at, :] = hid[m, :, columns].astype(jnp.float32)
            rt16[at, :] = routes[0, m]
            rw16[at, :] = rweights[0, m]
    chosen = rt16[...]
    chosen_weight = rw16[...]
    lanes = lax.broadcasted_iota(jnp.int32, (tall, 128), 1)
    table = jnp.zeros((tall, 128), jnp.float32)
    for k in range(chosen.shape[1]):
        table += jnp.where(chosen[:, k : k + 1] == lanes, chosen_weight[:, k : k + 1], 0.0)
    tab[...] = table

    def table_copy():
        return pltpu.make_async_remote_copy(
            src_ref=tab,
            dst_ref=tab_in,
            send_sem=t_send,
            recv_sem=t_recv,
            device_id={"section": 1},
            device_id_type=pl.DeviceIdType.MESH,
        )

    def back_copy():
        return pltpu.make_async_remote_copy(
            src_ref=xb,
            dst_ref=xb_in,
            send_sem=x_send,
            recv_sem=x_recv,
            device_id={"section": 0},
            device_id_type=pl.DeviceIdType.MESH,
        )

    def dispatch_copy(slot, other):
        return pltpu.make_async_remote_copy(
            src_ref=sbuf,
            dst_ref=disp.at[slot],
            send_sem=d_send.at[other],
            recv_sem=d_recv.at[slot],
            device_id={"expert": other},
            device_id_type=pl.DeviceIdType.MESH,
        )

    def return_copy(phase, slot, other):
        return pltpu.make_async_remote_copy(
            src_ref=pout.at[other],
            dst_ref=ret.at[phase, slot],
            send_sem=r_send.at[other],
            recv_sem=r_recv.at[phase, slot],
            device_id={"section": 1, "expert": other},
            device_id_type=pl.DeviceIdType.MESH,
        )

    def attend():
        loads[3].wait()
        loads[4].wait()
        positions = lax.broadcasted_iota(jnp.int32, (queries.shape[3], cache.shape[3]), 1)
        for m in range(micro):
            for r in range(rows):
                entries = c_v[m, r]
                scores = (
                    lax.dot_general(
                        q_v[m, r],
                        entries,
                        (((1,), (1,)), ((), ())),
                        preferred_element_type=jnp.float32,
                    )
                    * att_scale
                )
                scores = jnp.where(positions < lens[m, r], scores, -jnp.inf)
                expanded = jnp.exp(scores - jnp.max(scores, axis=1, keepdims=True))
                probs = (expanded / jnp.sum(expanded, axis=1, keepdims=True)).astype(jnp.bfloat16)
                ao_v[m, r] = jnp.dot(
                    probs, entries[:, :LAT], preferred_element_type=jnp.float32
                ).astype(jnp.bfloat16)
        pltpu.make_async_copy(ao_v, ao.at[0], out_sem).start()

    def combine(phase, weights, skip_own):
        total = xs[...]
        for e in range(EXPERTS):
            weight = weights[:, e : e + 1]

            def one(g, total):
                slot = e * group + g
                if skip_own:

                    @pl.when(slot != me)
                    def _():
                        return_copy(phase, slot, slot).wait_recv()

                else:
                    return_copy(phase, slot, slot).wait_recv()
                return total + weight * ret[phase, slot].astype(jnp.float32)

            if group == 1:
                total = one(0, total)
            else:
                total = lax.fori_loop(0, group, one, total)
        return total.astype(jnp.bfloat16)

    def emit(values):
        xs[...] = values.astype(jnp.float32)
        for q in range(FOLD):
            for m in range(micro):
                lo[0, m, :, pl.ds(q * fold, fold)] = xs[
                    pl.ds(q * per + m * rows, rows), :
                ].astype(jnp.bfloat16)

    pl.semaphore_wait(barrier, 2 * n - 1)

    @pl.when(sec == 0)
    def _():
        table_copy().start()

    @pl.when(sec == 1)
    def _():
        attend()
        table_copy().wait_recv()
        first = combine(0, tab_in[...], False)
        xb[...] = first
        back_copy().start()
        xs[...] = first.astype(jnp.float32)

    wide = xs[...]
    squares = jnp.sum(wide * wide, axis=1, keepdims=True)
    halves = jnp.broadcast_to(squares[: tall // 2] + squares[tall // 2 :], (tall // 2, 128))
    halves = halves + pltpu.roll(halves, per, 0)
    scale = lax.rsqrt(halves[:, :1] / width + 1e-06)
    scale = jnp.concatenate([scale, scale], axis=0)
    normed = (wide * scale * g16[...]).astype(jnp.bfloat16)
    sbuf[...] = normed
    disp[me] = normed

    def send(step):
        dispatch_copy(me, lax.rem(me + step + 1, n)).start()

    loop(n - 1, send)
    for copy in loads[:3]:
        copy.wait()

    chunk = 8
    flat = chunk * tall
    low_row = lax.broadcasted_iota(jnp.int32, (chunk, 2 * per, fold), 1) < per
    quarter = lax.rem(lax.broadcasted_iota(jnp.int32, (flat, 2 * hidden_units), 0), tall) // per

    def ffn(c):
        base = c * chunk

        def arrive(step):
            slot = base + step

            @pl.when(slot != me)
            def _():
                dispatch_copy(slot, slot).wait_recv()

        loop(chunk, arrive)
        block = disp[pl.ds(base, chunk)].reshape(flat, fold)
        total = jnp.zeros((flat, 2 * hidden_units), jnp.float32)
        for q in range(FOLD):
            part = jnp.dot(
                block, wgu_v[pl.ds(q * fold, fold), :], preferred_element_type=jnp.float32
            )
            total = jnp.where(quarter == q, part, total)
        total = total.reshape(chunk, 2, 2 * per, 2 * hidden_units)
        total = total[:, 0] + total[:, 1]
        total = (total + pltpu.roll(total, per, 1)).reshape(chunk * 2 * per, 2 * hidden_units)
        gate = total[:, :hidden_units]
        up = total[:, hidden_units:]
        activation = (gate / (1.0 + jnp.exp(-gate)) * up).astype(jnp.bfloat16)
        out = [
            jnp.dot(
                activation, wd_v[:, pl.ds(q * fold, fold)], preferred_element_type=jnp.float32
            ).reshape(chunk, 2 * per, fold)
            for q in range(FOLD)
        ]
        pout[pl.ds(base, chunk)] = jnp.concatenate(
            [jnp.where(low_row, out[0], out[1]), jnp.where(low_row, out[2], out[3])], axis=1
        ).astype(jnp.bfloat16)

        def give(step):
            other = base + step

            @pl.when((sec == 0) | (other != me))
            def _():
                return_copy(sec, me, other).start()

        loop(chunk, give)

    loop(n // chunk, ffn)

    @pl.when(sec == 0)
    def _():
        attend()
        back_copy().wait_recv()
        emit(xb_in[...])
        table_copy().wait_send()

    @pl.when(sec == 1)
    def _():
        ret[1, me] = pout[me]
        emit(combine(1, tab[...], True))
        back_copy().wait_send()

    def sent(step):
        dispatch_copy(me, lax.rem(me + step + 1, n)).wait_send()

    loop(n - 1, sent)

    def returned(step):
        @pl.when((sec == 0) | (step != me))
        def _():
            return_copy(sec, me, step).wait_send()

    loop(n, returned)
    pltpu.make_async_copy(ao_v, ao.at[0], out_sem).wait()


def shards(
    hidden_in,
    norm_gain,
    gate_weight,
    up_weight,
    down_weight,
    routes,
    route_weights,
    queries,
    latent_cache,
    lengths,
):
    n = lax.axis_size("expert")
    micro, rows, width = hidden_in.shape
    fold = width // FOLD
    tall = FOLD * micro * rows
    units = gate_weight.shape[2]
    heads = queries.shape[3]
    vmem = pl.BlockSpec(memory_space=pltpu.VMEM)
    smem = pl.BlockSpec(memory_space=pltpu.SMEM)
    far = pl.BlockSpec(memory_space=pl.ANY)
    dma = pltpu.SemaphoreType.DMA
    bf16, f32 = jnp.bfloat16, jnp.float32
    return pl.pallas_call(
        functools.partial(kernel, n),
        out_shape=(
            jax.ShapeDtypeStruct((1, micro, rows, width), bf16),
            jax.ShapeDtypeStruct((1, micro, rows, heads, LAT), bf16),
        ),
        in_specs=[vmem, vmem, far, far, far, vmem, vmem, far, far, smem],
        out_specs=(vmem, far),
        scratch_shapes=[
            pltpu.VMEM((tall, fold), f32),
            pltpu.VMEM((tall, fold), f32),
            pltpu.VMEM((tall, routes.shape[3]), jnp.int32),
            pltpu.VMEM((tall, routes.shape[3]), f32),
            pltpu.VMEM((tall, 128), f32),
            pltpu.VMEM((tall, 128), f32),
            pltpu.VMEM((tall, fold), bf16),
            pltpu.VMEM((n, tall, fold), bf16),
            pltpu.VMEM((n, tall, fold), bf16),
            pltpu.VMEM((2, n, tall, fold), bf16),
            pltpu.VMEM((tall, fold), bf16),
            pltpu.VMEM((tall, fold), bf16),
            pltpu.VMEM((width, 2 * units), bf16),
            pltpu.VMEM((units, width), bf16),
            pltpu.VMEM(queries.shape[1:], bf16),
            pltpu.VMEM(latent_cache.shape[1:], bf16),
            pltpu.VMEM((micro, rows, heads, LAT), bf16),
            dma((5,)),
            dma,
            dma((n,)),
            dma((n,)),
            dma((n,)),
            dma((2, n)),
            dma,
            dma,
            dma,
            dma,
        ],
        compiler_params=pltpu.CompilerParams(
            collective_id=0, has_side_effects=True, vmem_limit_bytes=56 * 1024 * 1024
        ),
    )(
        hidden_in,
        norm_gain,
        gate_weight,
        up_weight,
        down_weight,
        routes,
        route_weights,
        queries,
        latent_cache,
        lengths,
    )


def solution(mesh):
    return jax.shard_map(
        shards,
        mesh=mesh,
        in_specs=(
            P(None, ("groups", "expert"), None),
            P("section", None),
            P("section", None, "expert"),
            P("section", None, "expert"),
            P("section", "expert", None),
            P("section", None, ("groups", "expert"), None),
            P("section", None, ("groups", "expert"), None),
            P("section", None, ("groups", "expert"), None, None),
            P("section", None, ("groups", "expert"), None, None),
            P(None, ("groups", "expert")),
        ),
        out_specs=(
            P("section", None, ("groups", "expert"), None),
            P("section", None, ("groups", "expert"), None, None),
        ),
        check_vma=False,
    )
```

```python
import functools

import jax
import jax.numpy as jnp
from jax import lax
from jax.experimental import pallas as pl
from jax.experimental.pallas import tpu as pltpu
from jax.sharding import PartitionSpec as P

EXPERTS = 8
LAT = 512
FOLD = 4

att_scale = 0.07216878364870322


def loop(count, body):
    if count <= 8:
        for step in range(count):
            body(step)
    else:

        @pl.loop(0, count)
        def _(step):
            body(step)


def kernel(
    n,
    hid_far,
    gain_far,
    wg,
    wu,
    wd,
    routes_far,
    rweights_far,
    queries,
    cache,
    lens_far,
    lo,
    ao_v,
    hid,
    gain,
    routes,
    rweights,
    lens,
    xs,
    g16,
    rt16,
    rw16,
    tab,
    tab_in,
    sbuf,
    disp,
    pout,
    ret,
    xb,
    xb_in,
    wgu_v,
    wd_v,
    q_v,
    c_v,
    load_sem,
    d_send,
    d_recv,
    r_send,
    r_recv,
    t_send,
    t_recv,
    x_send,
    x_recv,
):
    sec = lax.axis_index("section")
    me = lax.axis_index("expert")
    micro, rows, width = hid.shape
    fold = width // FOLD
    per = micro * rows
    tall = FOLD * per
    hidden_units = wg.shape[2]
    group = n // EXPERTS

    barrier = pltpu.get_barrier_semaphore()

    def apart(step):
        return lax.rem(me + step + 1, n)

    @pl.when(sec == 0)
    def _():
        def greet(step):
            pl.semaphore_signal(
                barrier,
                inc=1,
                device_id={"expert": apart(step)},
                device_id_type=pl.DeviceIdType.MESH,
            )

        loop(n - 1, greet)

    pl.semaphore_signal(
        barrier, inc=1, device_id={"section": 1 - sec}, device_id_type=pl.DeviceIdType.MESH
    )

    loads = [
        pltpu.make_async_copy(wg.at[0], wgu_v.at[:, pl.ds(0, hidden_units)], load_sem.at[0]),
        pltpu.make_async_copy(
            wu.at[0], wgu_v.at[:, pl.ds(hidden_units, hidden_units)], load_sem.at[1]
        ),
        pltpu.make_async_copy(wd.at[0], wd_v, load_sem.at[2]),
        pltpu.make_async_copy(queries.at[0], q_v, load_sem.at[3]),
        pltpu.make_async_copy(cache.at[0], c_v, load_sem.at[4]),
        pltpu.make_async_copy(lens_far, lens, load_sem.at[5]),
    ]
    small = [
        pltpu.make_async_copy(far, near, load_sem.at[6 + place])
        for place, (far, near) in enumerate(
            [
                (hid_far, hid),
                (gain_far, gain),
                (routes_far, routes),
                (rweights_far, rweights),
            ]
        )
    ]
    for copy in small + loads:
        copy.start()

    for copy in small:
        copy.wait()

    for q in range(FOLD):
        columns = pl.ds(q * fold, fold)
        g16[pl.ds(q * per, per), :] = jnp.broadcast_to(gain[:, columns], (per, fold))
        for m in range(micro):
            at = pl.ds(q * per + m * rows, rows)
            xs[at, :] = hid[m, :, columns].astype(jnp.float32)
            rt16[at, :] = routes[0, m]
            rw16[at, :] = rweights[0, m]
    chosen = rt16[...]
    chosen_weight = rw16[...]
    lanes = lax.broadcasted_iota(jnp.int32, (tall, 128), 1)
    table = jnp.zeros((tall, 128), jnp.float32)
    for k in range(chosen.shape[1]):
        table += jnp.where(chosen[:, k : k + 1] == lanes, chosen_weight[:, k : k + 1], 0.0)
    tab[...] = table

    def table_copy():
        return pltpu.make_async_remote_copy(
            src_ref=tab,
            dst_ref=tab_in,
            send_sem=t_send,
            recv_sem=t_recv,
            device_id={"section": 1},
            device_id_type=pl.DeviceIdType.MESH,
        )

    def back_copy():
        return pltpu.make_async_remote_copy(
            src_ref=xb,
            dst_ref=xb_in,
            send_sem=x_send,
            recv_sem=x_recv,
            device_id={"section": 0},
            device_id_type=pl.DeviceIdType.MESH,
        )

    def dispatch_copy(slot, other):
        return pltpu.make_async_remote_copy(
            src_ref=sbuf,
            dst_ref=disp.at[slot],
            send_sem=d_send.at[other],
            recv_sem=d_recv.at[slot],
            device_id={"expert": other},
            device_id_type=pl.DeviceIdType.MESH,
        )

    def return_copy(phase, slot, other):
        return pltpu.make_async_remote_copy(
            src_ref=pout.at[other],
            dst_ref=ret.at[phase, slot],
            send_sem=r_send.at[other],
            recv_sem=r_recv.at[phase, slot],
            device_id={"section": 1, "expert": other},
            device_id_type=pl.DeviceIdType.MESH,
        )

    def attend():
        loads[3].wait()
        loads[4].wait()
        loads[5].wait()
        positions = lax.broadcasted_iota(jnp.int32, (queries.shape[3], cache.shape[3]), 1)
        for m in range(micro):
            for r in range(rows):
                entries = c_v[m, r]
                scores = (
                    lax.dot_general(
                        q_v[m, r],
                        entries,
                        (((1,), (1,)), ((), ())),
                        preferred_element_type=jnp.float32,
                    )
                    * att_scale
                )
                scores = jnp.where(positions < lens[m, r], scores, -jnp.inf)
                expanded = jnp.exp(scores - jnp.max(scores, axis=1, keepdims=True))
                probs = (expanded / jnp.sum(expanded, axis=1, keepdims=True)).astype(jnp.bfloat16)
                ao_v[0, m, r] = jnp.dot(
                    probs, entries[:, :LAT], preferred_element_type=jnp.float32
                ).astype(jnp.bfloat16)

    def combine(phase, weights, skip_own):
        total = xs[...]
        for e in range(EXPERTS):
            weight = weights[:, e : e + 1]

            def one(g, total):
                slot = e * group + g
                if skip_own:

                    @pl.when(slot != me)
                    def _():
                        return_copy(phase, slot, slot).wait_recv()

                else:
                    return_copy(phase, slot, slot).wait_recv()
                return total + weight * ret[phase, slot].astype(jnp.float32)

            if group == 1:
                total = one(0, total)
            else:
                total = lax.fori_loop(0, group, one, total)
        return total.astype(jnp.bfloat16)

    def emit(values):
        xs[...] = values.astype(jnp.float32)
        for q in range(FOLD):
            for m in range(micro):
                lo[0, m, :, pl.ds(q * fold, fold)] = xs[
                    pl.ds(q * per + m * rows, rows), :
                ].astype(jnp.bfloat16)

    def normalise():
        wide = xs[...]
        squares = jnp.sum(wide * wide, axis=1, keepdims=True)
        halves = jnp.broadcast_to(squares[: tall // 2] + squares[tall // 2 :], (tall // 2, 128))
        halves = halves + pltpu.roll(halves, per, 0)
        scale = lax.rsqrt(halves[:, :1] / width + 1e-06)
        scale = jnp.concatenate([scale, scale], axis=0)
        normed = (wide * scale * g16[...]).astype(jnp.bfloat16)
        sbuf[...] = normed
        disp[me] = normed

    @pl.when(sec == 0)
    def _():
        normalise()
        pl.semaphore_wait(barrier, n)

    @pl.when(sec == 1)
    def _():
        pl.semaphore_wait(barrier, 1)
        attend()
        table_copy().wait_recv()
        first = combine(0, tab_in[...], False)
        xb[...] = first
        xs[...] = first.astype(jnp.float32)
        normalise()

    def send(step):
        dispatch_copy(me, apart(step)).start()

    loop(n - 1, send)

    @pl.when(sec == 0)
    def _():
        table_copy().start()

    @pl.when(sec == 1)
    def _():
        back_copy().start()

    for copy in loads[:3]:
        copy.wait()

    chunk = 8
    flat = chunk * tall
    low_row = lax.broadcasted_iota(jnp.int32, (chunk, 2 * per, fold), 1) < per
    quarter = lax.rem(lax.broadcasted_iota(jnp.int32, (flat, 2 * hidden_units), 0), tall) // per

    def ffn(c):
        base = c * chunk

        def arrive(step):
            slot = base + step

            @pl.when(slot != me)
            def _():
                dispatch_copy(slot, slot).wait_recv()

        loop(chunk, arrive)
        block = disp[pl.ds(base, chunk)].reshape(flat, fold)
        total = jnp.zeros((flat, 2 * hidden_units), jnp.float32)
        for q in range(FOLD):
            part = jnp.dot(
                block, wgu_v[pl.ds(q * fold, fold), :], preferred_element_type=jnp.float32
            )
            total = jnp.where(quarter == q, part, total)
        total = total.reshape(chunk, 2, 2 * per, 2 * hidden_units)
        total = total[:, 0] + total[:, 1]
        total = (total + pltpu.roll(total, per, 1)).reshape(chunk * 2 * per, 2 * hidden_units)
        gate = total[:, :hidden_units]
        up = total[:, hidden_units:]
        activation = (gate / (1.0 + jnp.exp(-gate)) * up).astype(jnp.bfloat16)
        out = [
            jnp.dot(
                activation, wd_v[:, pl.ds(q * fold, fold)], preferred_element_type=jnp.float32
            ).reshape(chunk, 2 * per, fold)
            for q in range(FOLD)
        ]
        pout[pl.ds(base, chunk)] = jnp.concatenate(
            [jnp.where(low_row, out[0], out[1]), jnp.where(low_row, out[2], out[3])], axis=1
        ).astype(jnp.bfloat16)

        if n == chunk:
            for step in range(n - 1):
                return_copy(sec, me, apart(step)).start()

            @pl.when(sec == 0)
            def _():
                return_copy(sec, me, me).start()

        else:

            def give(step):
                other = base + step

                @pl.when((sec == 0) | (other != me))
                def _():
                    return_copy(sec, me, other).start()

            loop(chunk, give)

    loop(n // chunk, ffn)

    @pl.when(sec == 0)
    def _():
        attend()
        back_copy().wait_recv()
        emit(xb_in[...])
        table_copy().wait_send()

    @pl.when(sec == 1)
    def _():
        ret[1, me] = pout[me]
        emit(combine(1, tab[...], True))
        back_copy().wait_send()

    def sent(step):
        dispatch_copy(me, lax.rem(me + step + 1, n)).wait_send()

    loop(n - 1, sent)

    def returned(step):
        @pl.when((sec == 0) | (step != me))
        def _():
            return_copy(sec, me, step).wait_send()

    loop(n, returned)


def shards(
    hidden_in,
    norm_gain,
    gate_weight,
    up_weight,
    down_weight,
    routes,
    route_weights,
    queries,
    latent_cache,
    lengths,
):
    n = lax.axis_size("expert")
    micro, rows, width = hidden_in.shape
    fold = width // FOLD
    tall = FOLD * micro * rows
    units = gate_weight.shape[2]
    heads = queries.shape[3]
    vmem = pl.BlockSpec(memory_space=pltpu.VMEM)
    far = pl.BlockSpec(memory_space=pltpu.HBM)
    dma = pltpu.SemaphoreType.DMA
    bf16, f32 = jnp.bfloat16, jnp.float32
    return pl.pallas_call(
        functools.partial(kernel, n),
        out_shape=(
            pltpu.VMEM((1, micro, rows, width), bf16),
            pltpu.VMEM((1, micro, rows, heads, LAT), bf16),
        ),
        in_specs=[far] * 10,
        out_specs=(vmem, vmem),
        scratch_shapes=[
            pltpu.VMEM(hidden_in.shape, bf16),
            pltpu.VMEM(norm_gain.shape, f32),
            pltpu.VMEM(routes.shape, jnp.int32),
            pltpu.VMEM(route_weights.shape, f32),
            pltpu.SMEM(lengths.shape, jnp.int32),
            pltpu.VMEM((tall, fold), f32),
            pltpu.VMEM((tall, fold), f32),
            pltpu.VMEM((tall, routes.shape[3]), jnp.int32),
            pltpu.VMEM((tall, routes.shape[3]), f32),
            pltpu.VMEM((tall, 128), f32),
            pltpu.VMEM((tall, 128), f32),
            pltpu.VMEM((tall, fold), bf16),
            pltpu.VMEM((n, tall, fold), bf16),
            pltpu.VMEM((n, tall, fold), bf16),
            pltpu.VMEM((2, n, tall, fold), bf16),
            pltpu.VMEM((tall, fold), bf16),
            pltpu.VMEM((tall, fold), bf16),
            pltpu.VMEM((width, 2 * units), bf16),
            pltpu.VMEM((units, width), bf16),
            pltpu.VMEM(queries.shape[1:], bf16),
            pltpu.VMEM(latent_cache.shape[1:], bf16),
            dma((10,)),
            dma((n,)),
            dma((n,)),
            dma((n,)),
            dma((2, n)),
            dma,
            dma,
            dma,
            dma,
        ],
        compiler_params=pltpu.CompilerParams(
            collective_id=0, has_side_effects=True, vmem_limit_bytes=56 * 1024 * 1024
        ),
    )(
        hidden_in,
        norm_gain,
        gate_weight,
        up_weight,
        down_weight,
        routes,
        route_weights,
        queries,
        latent_cache,
        lengths,
    )


def solution(mesh):
    return jax.shard_map(
        shards,
        mesh=mesh,
        in_specs=(
            P(None, ("groups", "expert"), None),
            P("section", None),
            P("section", None, "expert"),
            P("section", None, "expert"),
            P("section", "expert", None),
            P("section", None, ("groups", "expert"), None),
            P("section", None, ("groups", "expert"), None),
            P("section", None, ("groups", "expert"), None, None),
            P("section", None, ("groups", "expert"), None, None),
            P(None, ("groups", "expert")),
        ),
        out_specs=(
            P("section", None, ("groups", "expert"), None),
            P("section", None, ("groups", "expert"), None, None),
        ),
        check_vma=False,
    )
```

```python
import functools

import jax
import jax.numpy as jnp
from jax import lax
from jax.experimental import pallas as pl
from jax.experimental.pallas import tpu as pltpu
from jax.sharding import PartitionSpec as P

EXPERTS = 8
LAT = 512
FOLD = 4

att_scale = 0.07216878364870322


def loop(count, body):
    if count <= 8:
        for step in range(count):
            body(step)
    else:

        @pl.loop(0, count)
        def _(step):
            body(step)


def kernel(
    n,
    hid_far,
    gain_far,
    wg,
    wu,
    wd,
    routes_far,
    rweights_far,
    queries,
    cache,
    lens_far,
    lo,
    ao_v,
    hid,
    gain,
    routes,
    rweights,
    lens,
    xs,
    g16,
    rt16,
    rw16,
    tab,
    tab_in,
    sbuf,
    disp,
    pout,
    ret,
    xb,
    xb_in,
    wgu_v,
    wd_v,
    q_v,
    c_v,
    load_sem,
    d_send,
    d_recv,
    r_send,
    r_recv,
    t_send,
    t_recv,
    x_send,
    x_recv,
):
    sec = lax.axis_index("section")
    me = lax.axis_index("expert")
    micro, rows, width = hid.shape
    fold = width // FOLD
    per = micro * rows
    tall = FOLD * per
    hidden_units = wg.shape[2]
    group = n // EXPERTS

    barrier = pltpu.get_barrier_semaphore()

    def apart(step):
        return lax.rem(me + step + 1, n)

    @pl.when(sec == 0)
    def _():
        def greet(step):
            pl.semaphore_signal(
                barrier,
                inc=1,
                device_id={"expert": apart(step)},
                device_id_type=pl.DeviceIdType.MESH,
            )

        loop(n - 1, greet)

    pl.semaphore_signal(
        barrier, inc=1, device_id={"section": 1 - sec}, device_id_type=pl.DeviceIdType.MESH
    )

    loads = [
        pltpu.make_async_copy(wg.at[0], wgu_v.at[:, pl.ds(0, hidden_units)], load_sem.at[0]),
        pltpu.make_async_copy(
            wu.at[0], wgu_v.at[:, pl.ds(hidden_units, hidden_units)], load_sem.at[1]
        ),
        pltpu.make_async_copy(wd.at[0], wd_v, load_sem.at[2]),
        pltpu.make_async_copy(queries.at[0], q_v, load_sem.at[3]),
        pltpu.make_async_copy(cache.at[0], c_v, load_sem.at[4]),
        pltpu.make_async_copy(lens_far, lens, load_sem.at[5]),
    ]
    small = [
        pltpu.make_async_copy(far, near, load_sem.at[6 + place])
        for place, (far, near) in enumerate(
            [
                (hid_far, hid),
                (gain_far, gain),
                (routes_far, routes),
                (rweights_far, rweights),
            ]
        )
    ]
    for copy in small + loads:
        copy.start()

    for copy in small:
        copy.wait()

    for q in range(FOLD):
        columns = pl.ds(q * fold, fold)
        g16[pl.ds(q * per, per), :] = jnp.broadcast_to(gain[:, columns], (per, fold))
        for m in range(micro):
            at = pl.ds(q * per + m * rows, rows)
            xs[at, :] = hid[m, :, columns].astype(jnp.float32)
            rt16[at, :] = routes[0, m]
            rw16[at, :] = rweights[0, m]
    chosen = rt16[...]
    chosen_weight = rw16[...]
    lanes = lax.broadcasted_iota(jnp.int32, (tall, 128), 1)
    table = jnp.zeros((tall, 128), jnp.float32)
    for k in range(chosen.shape[1]):
        table += jnp.where(chosen[:, k : k + 1] == lanes, chosen_weight[:, k : k + 1], 0.0)
    tab[...] = table

    def table_copy():
        return pltpu.make_async_remote_copy(
            src_ref=tab,
            dst_ref=tab_in,
            send_sem=t_send,
            recv_sem=t_recv,
            device_id={"section": 1},
            device_id_type=pl.DeviceIdType.MESH,
        )

    def back_copy():
        return pltpu.make_async_remote_copy(
            src_ref=xb,
            dst_ref=xb_in,
            send_sem=x_send,
            recv_sem=x_recv,
            device_id={"section": 0},
            device_id_type=pl.DeviceIdType.MESH,
        )

    def dispatch_copy(slot, other):
        return pltpu.make_async_remote_copy(
            src_ref=sbuf,
            dst_ref=disp.at[slot],
            send_sem=d_send.at[other],
            recv_sem=d_recv.at[slot],
            device_id={"expert": other},
            device_id_type=pl.DeviceIdType.MESH,
        )

    def return_copy(phase, slot, other):
        return pltpu.make_async_remote_copy(
            src_ref=pout.at[other],
            dst_ref=ret.at[phase, slot],
            send_sem=r_send.at[other],
            recv_sem=r_recv.at[phase, slot],
            device_id={"section": 1, "expert": other},
            device_id_type=pl.DeviceIdType.MESH,
        )

    def attend():
        loads[3].wait()
        loads[4].wait()
        loads[5].wait()
        positions = lax.broadcasted_iota(jnp.int32, (queries.shape[3], cache.shape[3]), 1)
        for m in range(micro):
            for r in range(rows):
                entries = c_v[m, r]
                scores = (
                    lax.dot_general(
                        q_v[m, r],
                        entries,
                        (((1,), (1,)), ((), ())),
                        preferred_element_type=jnp.float32,
                    )
                    * att_scale
                )
                scores = jnp.where(positions < lens[m, r], scores, -jnp.inf)
                expanded = jnp.exp(scores - jnp.max(scores, axis=1, keepdims=True))
                probs = (expanded / jnp.sum(expanded, axis=1, keepdims=True)).astype(jnp.bfloat16)
                ao_v[0, m, r] = jnp.dot(
                    probs, entries[:, :LAT], preferred_element_type=jnp.float32
                ).astype(jnp.bfloat16)

    def combine(phase, weights, skip_own):
        total = xs[...]
        for e in range(EXPERTS):
            weight = weights[:, e : e + 1]

            def one(g, total):
                slot = e * group + g
                if skip_own:

                    @pl.when(slot != me)
                    def _():
                        return_copy(phase, slot, slot).wait_recv()

                else:
                    return_copy(phase, slot, slot).wait_recv()
                return total + weight * ret[phase, slot].astype(jnp.float32)

            if group == 1:
                total = one(0, total)
            else:
                total = lax.fori_loop(0, group, one, total)
        return total.astype(jnp.bfloat16)

    def emit(values):
        xs[...] = values.astype(jnp.float32)
        for q in range(FOLD):
            for m in range(micro):
                lo[0, m, :, pl.ds(q * fold, fold)] = xs[
                    pl.ds(q * per + m * rows, rows), :
                ].astype(jnp.bfloat16)

    def normalise():
        wide = xs[...]
        squares = jnp.sum(wide * wide, axis=1, keepdims=True)
        halves = jnp.broadcast_to(squares[: tall // 2] + squares[tall // 2 :], (tall // 2, 128))
        halves = halves + pltpu.roll(halves, per, 0)
        scale = lax.rsqrt(halves[:, :1] / width + 1e-06)
        scale = jnp.concatenate([scale, scale], axis=0)
        normed = (wide * scale * g16[...]).astype(jnp.bfloat16)
        sbuf[...] = normed
        disp[me] = normed

    @pl.when(sec == 0)
    def _():
        normalise()
        pl.semaphore_wait(barrier, n)

    @pl.when(sec == 1)
    def _():
        pl.semaphore_wait(barrier, 1)
        attend()
        table_copy().wait_recv()
        first = combine(0, tab_in[...], False)
        xb[...] = first
        xs[...] = first.astype(jnp.float32)
        normalise()

    def send(step):
        dispatch_copy(me, apart(step)).start()

    loop(n - 1, send)

    @pl.when(sec == 0)
    def _():
        table_copy().start()

    @pl.when(sec == 1)
    def _():
        back_copy().start()

    for copy in loads[:3]:
        copy.wait()

    chunk = 8
    flat = chunk * tall
    low_row = lax.broadcasted_iota(jnp.int32, (chunk, 2 * per, fold), 1) < per
    quarter = lax.rem(lax.broadcasted_iota(jnp.int32, (flat, 2 * hidden_units), 0), tall) // per

    def ffn(c):
        base = c * chunk

        def arrive(step):
            slot = base + step

            @pl.when(slot != me)
            def _():
                dispatch_copy(slot, slot).wait_recv()

        loop(chunk, arrive)
        block = disp[pl.ds(base, chunk)].reshape(flat, fold)
        total = jnp.zeros((flat, 2 * hidden_units), jnp.float32)
        for q in range(FOLD):
            part = jnp.dot(
                block, wgu_v[pl.ds(q * fold, fold), :], preferred_element_type=jnp.float32
            )
            total = jnp.where(quarter == q, part, total)
        total = total.reshape(chunk, 2, 2 * per, 2 * hidden_units)
        total = total[:, 0] + total[:, 1]
        total = (total + pltpu.roll(total, per, 1)).reshape(chunk * 2 * per, 2 * hidden_units)
        gate = total[:, :hidden_units]
        up = total[:, hidden_units:]
        activation = (gate / (1.0 + jnp.exp(-gate)) * up).astype(jnp.bfloat16)
        out = [
            jnp.dot(
                activation, wd_v[:, pl.ds(q * fold, fold)], preferred_element_type=jnp.float32
            ).reshape(chunk, 2 * per, fold)
            for q in range(FOLD)
        ]
        pout[pl.ds(base, chunk)] = jnp.concatenate(
            [jnp.where(low_row, out[0], out[1]), jnp.where(low_row, out[2], out[3])], axis=1
        ).astype(jnp.bfloat16)

        if n == chunk:
            for step in range(n - 1):
                return_copy(sec, me, apart(step)).start()

            @pl.when(sec == 0)
            def _():
                return_copy(sec, me, me).start()

        else:

            def give(step):
                other = base + step

                @pl.when((sec == 0) | (other != me))
                def _():
                    return_copy(sec, me, other).start()

            loop(chunk, give)

    loop(n // chunk, ffn)

    @pl.when(sec == 0)
    def _():
        attend()
        back_copy().wait_recv()
        emit(xb_in[...])
        table_copy().wait_send()

    @pl.when(sec == 1)
    def _():
        ret[1, me] = pout[me]
        emit(combine(1, tab[...], True))
        back_copy().wait_send()

    def sent(step):
        dispatch_copy(me, lax.rem(me + step + 1, n)).wait_send()

    loop(n - 1, sent)

    def returned(step):
        @pl.when((sec == 0) | (step != me))
        def _():
            return_copy(sec, me, step).wait_send()

    loop(n, returned)


def hand_out(layer, attention, layer_to, attention_to, sems):
    copies = [
        pltpu.make_async_copy(attention, attention_to, sems.at[0]),
        pltpu.make_async_copy(layer, layer_to, sems.at[1]),
    ]
    for copy in copies:
        copy.start()
    for copy in copies:
        copy.wait()


def shards(
    hidden_in,
    norm_gain,
    gate_weight,
    up_weight,
    down_weight,
    routes,
    route_weights,
    queries,
    latent_cache,
    lengths,
):
    n = lax.axis_size("expert")
    micro, rows, width = hidden_in.shape
    fold = width // FOLD
    tall = FOLD * micro * rows
    units = gate_weight.shape[2]
    heads = queries.shape[3]
    vmem = pl.BlockSpec(memory_space=pltpu.VMEM)
    far = pl.BlockSpec(memory_space=pltpu.HBM)
    dma = pltpu.SemaphoreType.DMA
    bf16, f32 = jnp.bfloat16, jnp.float32
    results = pl.pallas_call(
        functools.partial(kernel, n),
        out_shape=(
            pltpu.VMEM((1, micro, rows, width), bf16),
            pltpu.VMEM((1, micro, rows, heads, LAT), bf16),
        ),
        in_specs=[far] * 10,
        out_specs=(vmem, vmem),
        scratch_shapes=[
            pltpu.VMEM(hidden_in.shape, bf16),
            pltpu.VMEM(norm_gain.shape, f32),
            pltpu.VMEM(routes.shape, jnp.int32),
            pltpu.VMEM(route_weights.shape, f32),
            pltpu.SMEM(lengths.shape, jnp.int32),
            pltpu.VMEM((tall, fold), f32),
            pltpu.VMEM((tall, fold), f32),
            pltpu.VMEM((tall, routes.shape[3]), jnp.int32),
            pltpu.VMEM((tall, routes.shape[3]), f32),
            pltpu.VMEM((tall, 128), f32),
            pltpu.VMEM((tall, 128), f32),
            pltpu.VMEM((tall, fold), bf16),
            pltpu.VMEM((n, tall, fold), bf16),
            pltpu.VMEM((n, tall, fold), bf16),
            pltpu.VMEM((2, n, tall, fold), bf16),
            pltpu.VMEM((tall, fold), bf16),
            pltpu.VMEM((tall, fold), bf16),
            pltpu.VMEM((width, 2 * units), bf16),
            pltpu.VMEM((units, width), bf16),
            pltpu.VMEM(queries.shape[1:], bf16),
            pltpu.VMEM(latent_cache.shape[1:], bf16),
            dma((10,)),
            dma((n,)),
            dma((n,)),
            dma((n,)),
            dma((2, n)),
            dma,
            dma,
            dma,
            dma,
        ],
        compiler_params=pltpu.CompilerParams(
            collective_id=0, has_side_effects=True, vmem_limit_bytes=56 * 1024 * 1024
        ),
    )(
        hidden_in,
        norm_gain,
        gate_weight,
        up_weight,
        down_weight,
        routes,
        route_weights,
        queries,
        latent_cache,
        lengths,
    )
    return pl.pallas_call(
        hand_out,
        out_shape=tuple(jax.ShapeDtypeStruct(value.shape, value.dtype) for value in results),
        in_specs=[vmem] * 2,
        out_specs=(far, far),
        scratch_shapes=[dma((2,))],
    )(*[pltpu.with_memory_space_constraint(value, pltpu.VMEM) for value in results])


def solution(mesh):
    return jax.shard_map(
        shards,
        mesh=mesh,
        in_specs=(
            P(None, ("groups", "expert"), None),
            P("section", None),
            P("section", None, "expert"),
            P("section", None, "expert"),
            P("section", "expert", None),
            P("section", None, ("groups", "expert"), None),
            P("section", None, ("groups", "expert"), None),
            P("section", None, ("groups", "expert"), None, None),
            P("section", None, ("groups", "expert"), None, None),
            P(None, ("groups", "expert")),
        ),
        out_specs=(
            P("section", None, ("groups", "expert"), None),
            P("section", None, ("groups", "expert"), None, None),
        ),
        check_vma=False,
    )
```
